128 devices in a mesh: fsdp: 16 (over y, x), tp: 8 (over z, core).
Axes of the slice: x: 4, y: 4, z: 4, core: 2. Of those that a mesh axis runs over, the one named last changes fastest.
Arguments:
- old_codes: bfloat16 [32768, 8192], P(('fsdp', 'tp')), may hold values from -448 to 448
- old_scales: bfloat16 [256, 64], P(('fsdp', 'tp')), may hold values from 4.9829483e-05 to 0.00049972534
- old_offsets: int32 [129], replicated, may hold values from 0 to 14336, as said below
- tokens: bfloat16 [4096, 8192], P('fsdp'), may hold values from -6 to 6
- cotangent: bfloat16 [4096, 14336], P('fsdp', 'tp'), may hold values from -0.1796875 to 0.1796875
Outputs:
- projected: bfloat16 [4096, 14336], P('fsdp', 'tp')
- grad: float32 [8192, 14336], P('fsdp', 'tp')
The draws below stay inside these ranges and needn't reach their ends.
Inputs may be any that keep to these rules, and one draw needn't show every extreme that they name: old_offsets never falls, starts at 0, ends at 14336 and holds multiples of 128; owner o is the device at position o of fsdp+tp and holds saved rows old_offsets[o] to old_offsets[o + 1] - 1 in the first rows of its 256 rows of old_codes and its scales in the first rows of its 2 rows of old_scales; no owner holds more than 256 rows and some owner holds exactly 256; old_offsets[k * 16] = k * 1792 for every k.
All inputs are finite; a program needn't handle non-finite values.
Results may differ from the reference program's by a relative error of at most 0.0049.
Values may be sent and summed in bfloat16 or wider, within the bound.
No kernel may reach another device: no remote copies, remote signals or barrier semaphores. Data moves between devices by JAX's collectives and lax.ppermute only.
A program may use at most 192 MiB of HBM per device.

```python
import math
import jax
import jax.numpy as jnp
from jax import lax

D = 8192
FF = 14336
QB = 128
TOKENS = 4096
OWNERS = 128
CAPB = 2
CAP = 256
N_FSDP = 16
N_TP = 8


def draw_old_offsets(key, part):
    key = jax.random.fold_in(key, 11)
    needed = FF // (QB * N_TP)
    others_count = N_FSDP - 1

    def group_counts(group_key):
        key_full, key_perm = jax.random.split(group_key)
        full_owner = jax.random.randint(key_full, (), 0, N_FSDP)
        shuffled = jax.random.permutation(key_perm, others_count * CAPB)
        chosen = shuffled[:needed - CAPB] // CAPB
        other_counts = jnp.sum((chosen[:, None] == jnp.arange(others_count)[None, :]).astype(jnp.int32), axis=0)
        positions = jnp.arange(N_FSDP)
        other_index = jnp.clip(positions - (positions > full_owner).astype(jnp.int32), 0, others_count - 1)
        return jnp.where(positions == full_owner, CAPB, other_counts[other_index]).astype(jnp.int32)
    counts = jax.vmap(group_counts)(jax.random.split(key, N_TP)).reshape(-1)
    ends = jnp.cumsum(counts) * QB
    return jnp.concatenate([jnp.zeros((1,), jnp.int32), ends.astype(jnp.int32)])


def block_levels(stream_key, extent, pieces, low, high):
    def one(position, parts):
        draws = jax.random.uniform(jax.random.fold_in(jax.random.fold_in(stream_key, 6), position), (parts,), jnp.float32, low / len(pieces), high / len(pieces))
        return jnp.repeat(jnp.exp(draws), extent[position] // parts).reshape((-1,) + (1,) * (len(extent) - position - 1))

    loudness = one(*pieces[0])
    for cut in pieces[1:]:
        loudness = loudness * one(*cut)
    return loudness


def bell_draw(stream_key, dims, scale, limit, cuts=(), kind=jnp.bfloat16):
    array = scale * jax.random.normal(stream_key, dims, jnp.float32)
    if cuts:
        array = array * block_levels(stream_key, dims, cuts, -0.22, 0.18)
    return jnp.clip(array, -limit, limit).astype(kind)


def setup_inputs(seed: int = 0) -> dict:
    streams_of = jax.random.split(jax.random.key(seed), 6)
    old_codes = bell_draw(streams_of[0], (OWNERS * CAP, D), 64.0, 448.0, ((0, 128),))
    old_scales = jnp.clip(jnp.exp(math.log(0.00049972534) - 2.3054518 * jax.random.uniform(streams_of[1], (OWNERS * CAPB, D // QB), jnp.float32) ** block_levels(streams_of[1], (OWNERS * CAPB, D // QB), ((0, 128),), -0.2, 0.2)), 4.982948303222656e-05, 0.00049972534).astype(jnp.bfloat16)
    old_offsets = draw_old_offsets(jax.random.fold_in(streams_of[5], 71), 0)
    tokens = bell_draw(streams_of[3], (TOKENS, D), 1.0, 6.0, ((0, 16),))
    cotangent = bell_draw(streams_of[4], (TOKENS, FF), 0.03, 0.1796875, ((0, 16), (1, 8)))
    return dict(old_codes=old_codes, old_scales=old_scales, old_offsets=old_offsets, tokens=tokens, cotangent=cotangent)


def reference(old_codes, old_scales, old_offsets, tokens, cotangent):
    row_ids = jnp.arange(FF, dtype=jnp.int32)
    starts = old_offsets[:OWNERS]
    owner_ids = (jnp.sum((starts[None, :] <= row_ids[:, None]).astype(jnp.int32), axis=1) - 1).astype(jnp.int32)
    slot_ids = (owner_ids * CAP + row_ids - old_offsets[owner_ids]).astype(jnp.int32)
    picked = old_codes[slot_ids]
    picked_scales = old_scales[slot_ids // QB]
    scaled = picked.astype(jnp.float32).reshape(FF, D // QB, QB) * picked_scales.astype(jnp.float32)[:, :, None]
    weight = scaled.reshape(FF, D).astype(jnp.bfloat16)
    summed = lax.dot_general(tokens, weight, (((1,), (1,)), ((), ())), preferred_element_type=jnp.float32)
    projected = summed.astype(jnp.bfloat16)
    grad = jnp.dot(tokens.T, cotangent, preferred_element_type=jnp.float32)
    return projected, grad
```

```python
import math

import jax
import jax.numpy as jnp
from jax import lax
from jax.experimental import pallas as pl
from jax.experimental.pallas import tpu as pltpu
from jax.sharding import Mesh, PartitionSpec as P

AXES = ("y", "x", "z", "c")
RING = 4
NEAR_LAST = (2, 1, 3)
PARAMS = pltpu.CompilerParams(vmem_limit_bytes=56 << 20)


def swap(array, axis, s):
    return lax.ppermute(array, axis, [(i, i ^ s) for i in range(RING)])


def exchange(parts, axis):
    got = [parts[0]] + [None] * (RING - 1)
    for s in NEAR_LAST:
        got[s] = swap(parts[s], axis, s)
    return got


def pick(array, index, axis=0):
    return lax.dynamic_index_in_dim(array, index, axis, keepdims=False)


def all_to_all(array, axis):
    return lax.all_to_all(array, axis, 0, 0, tiled=True)


def cut_kernel(place_ref, tokens_ref, out_ref):
    part = out_ref.shape[2]
    for x in range(RING):
        out_ref[x] = tokens_ref[:, x * part:(x + 1) * part]


def cut_tokens(tokens, c):
    rows, width = tokens.shape
    quarter = width // RING
    part = quarter // RING
    return pl.pallas_call(
        cut_kernel,
        grid_spec=pltpu.PrefetchScalarGridSpec(
            num_scalar_prefetch=1,
            grid=(RING,),
            in_specs=[pl.BlockSpec((rows // 2, quarter), lambda q, place: (place[0], q))],
            out_specs=pl.BlockSpec((RING, rows // 2, part), lambda q, place: (0, 0, q)),
        ),
        out_shape=jax.ShapeDtypeStruct((RING, rows // 2, quarter), tokens.dtype),
        compiler_params=PARAMS,
        name="cut_tokens",
    )(c[None], tokens)


def dequantize_kernel(place_ref, codes_ref, scales_ref, first_ref, *second_refs):
    step = pl.program_id(0)
    part = first_ref.shape[-1]
    block = first_ref.shape[-2]

    def values(slot, x):
        cols = slice(x * part, (x + 1) * part)
        codes = codes_ref[slot * block:(slot + 1) * block, cols].astype(jnp.float32)
        return (codes * scales_ref[slot:slot + 1, cols]).astype(jnp.bfloat16)

    for x in range(RING):
        first_ref[x, 0] = values(0, x)
    for s, ref in enumerate(second_refs):
        @pl.when(step == s)
        def _():
            for x in range(RING):
                ref[x] = values(1, x)


def dequantize(codes, scales, z):
    capacity, width = codes.shape
    slots, col_blocks = scales.shape
    block = capacity // slots
    quarter = width // RING
    part = quarter // RING
    spread = jnp.repeat(scales.astype(jnp.float32), width // col_blocks, axis=1)
    return pl.pallas_call(
        dequantize_kernel,
        grid_spec=pltpu.PrefetchScalarGridSpec(
            num_scalar_prefetch=1,
            grid=(RING,),
            in_specs=[
                pl.BlockSpec((capacity, quarter), lambda i, place: (0, place[0] ^ i)),
                pl.BlockSpec((slots, quarter), lambda i, place: (0, place[0] ^ i)),
            ],
            out_specs=[pl.BlockSpec((RING, 1, block, part), lambda i, place: (0, place[0] ^ i, 0, 0))]
            + [pl.BlockSpec((RING, block, part), lambda i, place: (0, 0, 0))] * RING,
        ),
        out_shape=[jax.ShapeDtypeStruct((RING, RING, block, part), jnp.bfloat16)]
        + [jax.ShapeDtypeStruct((RING, block, part), jnp.bfloat16)] * RING,
        compiler_params=PARAMS,
        name="dequantize",
    )(z[None], codes, spread)


def gather_kernel(kind_ref, index_ref, half_ref, *refs):
    sources, outs = refs[:6], refs[6:10]
    rows = math.gcd(outs[0].shape[0], sources[0].shape[1])
    count = outs[0].shape[0] // rows
    for s, out_ref in enumerate(outs):
        for i in range(count):
            n = s * count + i
            half = pl.ds(pl.multiple_of(half_ref[n] * rows, rows), rows)
            for kind, source in enumerate(sources):
                @pl.when(kind_ref[n] == kind)
                def _():
                    out_ref[i * rows:(i + 1) * rows, :] = source[index_ref[n], half, :]


def gather(kind, index, half, sources, hidden):
    part = sources[0].shape[-1]
    return pl.pallas_call(
        gather_kernel,
        grid_spec=pltpu.PrefetchScalarGridSpec(
            num_scalar_prefetch=3,
            grid=(1,),
            in_specs=[pl.BlockSpec(a.shape, lambda i, *_: (0, 0, 0)) for a in sources],
            out_specs=[pl.BlockSpec((hidden, part), lambda i, *_: (0, 0))] * RING,
        ),
        out_shape=[jax.ShapeDtypeStruct((hidden, part), sources[0].dtype)] * RING,
        compiler_params=PARAMS,
        name="gather_blocks",
    )(kind, index, half, *sources)


def weight_rows(old_codes, old_scales, old_offsets, local_hidden, cot):
    y, x, z, c = (lax.axis_index(a) for a in AXES)
    owners = RING * RING
    slots = old_scales.shape[0]
    block = old_codes.shape[0] // slots
    hidden = local_hidden // RING
    first, *second = dequantize(old_codes, old_scales, z)
    part = first.shape[-1]

    second = jnp.stack(exchange(second, "z"), axis=1)
    first = all_to_all(first, "x")
    firsts = exchange([pick(first, z ^ s, 1) for s in range(RING)], "z")
    second = all_to_all(second, "x")
    second, cot = lax.optimization_barrier((second, cot))
    give = [lax.dynamic_slice_in_dim(a, 2 * (1 - c), 2, 0) for a in firsts]
    give = give + [lax.dynamic_slice_in_dim(second, 2 * (1 - c), 2, 0).reshape(2 * RING, block, part)]
    other = lax.ppermute(jnp.concatenate(give), "c", [(0, 1), (1, 0)])

    group = 2 * y + c
    rows = math.gcd(hidden, block)
    count = hidden // rows
    n = jnp.arange(RING * count, dtype=jnp.int32)
    row = group * local_hidden + (z ^ (n // count)) * hidden + rows * (n % count)
    starts = old_offsets[:-1]
    before = (starts[None, :] <= row[:, None]).astype(jnp.int32)
    owner = jnp.sum(before, axis=1) - 1
    start = jnp.max(jnp.where(before == 1, starts[None, :], 0), axis=1)
    member = owner - group * owners
    low, zs, cs = member >> 3, (member >> 1) & 3, member & 1
    slot = (row - start) // block
    half = (row - start) % block // rows
    s = zs ^ z
    kind = jnp.where(cs != c, RING + 1, jnp.where(slot == 0, s, RING))
    index = jnp.where(
        cs != c,
        jnp.where(slot == 0, s * 2 + low, 2 * RING + low * RING + s),
        jnp.where(slot == 0, 2 * c + low, (2 * c + low) * RING + s),
    )
    sources = firsts + [second.reshape(owners, block, part), other]
    return gather(kind, index, half, sources, hidden), cot


def project_kernel(place_ref, tokens_ref, *refs):
    out_ref = refs[-1]
    pieces, hidden, share = out_ref.shape
    total = None
    for s, weight_ref in enumerate(refs[:-1]):
        part = weight_ref.shape[1]
        start = pl.multiple_of((place_ref[1] ^ s) * part, part)
        rows = tokens_ref[:, 0, :, pl.ds(start, part)].reshape(pieces * share, part)
        product = lax.dot_general(
            weight_ref[...], rows, (((1,), (1,)), ((), ())), preferred_element_type=jnp.float32
        )
        total = product if total is None else total + product
    for i in range(pieces):
        out_ref[i] = total[:, i * share:(i + 1) * share].astype(out_ref.dtype)


def project(tokens, weights, x, z):
    pieces, _, share, quarter = tokens.shape
    steps = 2
    hidden, part = weights[0].shape
    rows = pieces * share // RING
    return pl.pallas_call(
        project_kernel,
        grid_spec=pltpu.PrefetchScalarGridSpec(
            num_scalar_prefetch=1,
            grid=(steps,),
            in_specs=[
                pl.BlockSpec((pieces // steps, 1, share, quarter), lambda i, place: (i, place[0], 0, 0))
            ]
            + [pl.BlockSpec((hidden, part), lambda i, place: (0, 0))] * RING,
            out_specs=pl.BlockSpec((RING // steps, hidden, rows), lambda i, place: (i, 0, 0)),
        ),
        out_shape=jax.ShapeDtypeStruct((RING, hidden, rows), jnp.bfloat16),
        compiler_params=PARAMS,
        name="project",
    )(jnp.stack([x, z]), tokens, *weights)


def grad_kernel(place_ref, tokens_ref, *refs):
    cots, outs, total_ref, cot_ref = refs[:RING], refs[RING:2 * RING], refs[2 * RING], refs[2 * RING + 1]
    step = pl.program_id(0)
    rows = cots[0].shape[2]
    part = outs[0].shape[1]
    for s, ref in enumerate(cots):
        @pl.when(step == s)
        def _():
            for t in range(RING):
                start = pl.multiple_of((place_ref[0] ^ t) * rows, rows)
                cot_ref[:, pl.ds(start, rows)] = ref[t]
    product = lax.dot_general(
        cot_ref[...], tokens_ref[...].reshape(cot_ref.shape[1], tokens_ref.shape[-1]),
        (((1,), (0,)), ((), ())), preferred_element_type=jnp.float32,
    )

    @pl.when(step == 0)
    def _():
        total_ref[...] = product

    @pl.when(step > 0)
    def _():
        total_ref[...] += product

    @pl.when(step == pl.num_programs(0) - 1)
    def _():
        for s, ref in enumerate(outs):
            start = pl.multiple_of((place_ref[0] ^ s) * part, part)
            ref[...] = total_ref[:, pl.ds(start, part)].astype(ref.dtype)


def gradient(tokens, cots, y, x):
    pieces, _, share, quarter = tokens.shape
    part = quarter // RING
    _, hidden, rows = cots[0].shape
    return pl.pallas_call(
        grad_kernel,
        grid_spec=pltpu.PrefetchScalarGridSpec(
            num_scalar_prefetch=1,
            grid=(RING,),
            in_specs=[pl.BlockSpec((pieces, 1, share, quarter), lambda i, place: (0, place[1] ^ i, 0, 0))]
            + [pl.BlockSpec((RING, hidden, rows), lambda i, place: (0, 0, 0))] * RING,
            out_specs=[pl.BlockSpec((hidden, part), lambda i, place: (0, 0))] * RING,
            scratch_shapes=[
                pltpu.VMEM((hidden, quarter), jnp.float32),
                pltpu.VMEM((hidden, RING * rows), jnp.bfloat16),
            ],
        ),
        out_shape=[jax.ShapeDtypeStruct((hidden, part), jnp.bfloat16)] * RING,
        compiler_params=PARAMS,
        name="gradient",
    )(jnp.stack([y, x]), tokens, *cots)


def assemble_kernel(place_ref, *refs):
    pieces, out_ref, all_ref = refs[:RING], refs[RING], refs[RING + 1]
    hidden = pieces[0].shape[0]
    for s, ref in enumerate(pieces):
        start = pl.multiple_of((place_ref[0] ^ s) * hidden, hidden)
        all_ref[pl.ds(start, hidden), :] = ref[...].astype(jnp.float32)
    out_ref[...] = all_ref[...].T.astype(out_ref.dtype)


def assemble(pieces, me, dtype):
    hidden, rows = pieces[0].shape
    lanes = min(rows, 128)
    return pl.pallas_call(
        assemble_kernel,
        grid_spec=pltpu.PrefetchScalarGridSpec(
            num_scalar_prefetch=1,
            grid=(rows // lanes,),
            in_specs=[pl.BlockSpec((hidden, lanes), lambda i, place: (0, i))] * RING,
            out_specs=pl.BlockSpec((lanes, RING * hidden), lambda i, place: (i, 0)),
            scratch_shapes=[pltpu.VMEM((RING * hidden, lanes), jnp.float32)],
        ),
        out_shape=jax.ShapeDtypeStruct((rows, RING * hidden), dtype),
        compiler_params=PARAMS,
        name="assemble",
    )(me[None], *pieces)


def on_device(old_codes, old_scales, old_offsets, tokens, cotangent):
    y, x, z, c = (lax.axis_index(a) for a in AXES)
    local_tokens, width = tokens.shape
    local_hidden = cotangent.shape[1]
    hidden = local_hidden // RING

    with jax.named_scope("tokens"):
        every = lax.all_gather(all_to_all(cut_tokens(tokens, c), "x"), ("y", "c"))

    with jax.named_scope("cotangent"):
        cut = cotangent.T.reshape(RING, hidden, local_tokens)
        cot = jnp.stack(exchange([pick(cut, y ^ s) for s in range(RING)], "y"))

    with jax.named_scope("weight"):
        weights, cot = weight_rows(old_codes, old_scales, old_offsets, local_hidden, cot)
        weights = exchange(weights, "z")

    with jax.named_scope("grad"):
        cots = exchange([cot] * RING, "x")
        grad = assemble(exchange(gradient(every, cots, y, x), "y"), y, jnp.float32)

    with jax.named_scope("projected"):
        parts = [None] * RING
        for s in NEAR_LAST:
            parts[s] = swap(project(every, weights, x ^ s, z), "x", s)
        parts[0] = project(every, weights, x, z)
        total = sum(p.astype(jnp.float32) for p in parts).astype(jnp.bfloat16)
        done = []
        for s in range(RING):
            pairs = [(a * RING + b, (b ^ s) * RING + a) for a in range(RING) for b in range(RING)]
            done.append(lax.ppermute(pick(total, z ^ s), ("y", "z"), pairs))
        projected = assemble(done, y, jnp.bfloat16)
    return (projected, grad)


def solution(mesh):
    devices = mesh.devices.reshape(RING, RING, RING, 2)
    split = Mesh(devices, AXES)
    fsdp, tp = ("y", "x"), ("z", "c")
    placed = (P(fsdp + tp, None), P(fsdp + tp, None), P(), P(fsdp, None), P(fsdp, tp))
    return jax.shard_map(
        on_device,
        mesh=split,
        in_specs=placed,
        out_specs=(P(fsdp, tp), P(fsdp, tp)),
        check_vma=False,
    )
```

```python
import math

import jax
import jax.numpy as jnp
from jax import lax
from jax.experimental import pallas as pl
from jax.experimental.pallas import tpu as pltpu
from jax.sharding import Mesh, PartitionSpec as P

AXES = ("y", "x", "z", "c")
RING = 4
NEAR_LAST = (2, 1, 3)
PARAMS = pltpu.CompilerParams(vmem_limit_bytes=56 << 20)


def swap(array, axis, s):
    return lax.ppermute(array, axis, [(i, i ^ s) for i in range(RING)])


def exchange(parts, axis):
    got = [parts[0]] + [None] * (RING - 1)
    for s in NEAR_LAST:
        got[s] = swap(parts[s], axis, s)
    return got


def pick(array, index, axis=0):
    return lax.dynamic_index_in_dim(array, index, axis, keepdims=False)


def all_to_all(array, axis):
    return lax.all_to_all(array, axis, 0, 0, tiled=True)


def cut_kernel(place_ref, tokens_ref, out_ref):
    part = out_ref.shape[2]
    for x in range(RING):
        out_ref[x] = tokens_ref[:, x * part:(x + 1) * part]


def cut_tokens(tokens, place, rows):
    width = tokens.shape[1]
    quarter = width // RING
    part = quarter // RING
    return pl.pallas_call(
        cut_kernel,
        grid_spec=pltpu.PrefetchScalarGridSpec(
            num_scalar_prefetch=1,
            grid=(RING,),
            in_specs=[pl.BlockSpec((rows, quarter), lambda q, place: (place[0], q))],
            out_specs=pl.BlockSpec((RING, rows, part), lambda q, place: (0, 0, q)),
        ),
        out_shape=jax.ShapeDtypeStruct((RING, rows, quarter), tokens.dtype),
        compiler_params=PARAMS,
        name="cut_tokens",
    )(place[None], tokens)


def dequantize_kernel(place_ref, codes_ref, scales_ref, first_ref, *second_refs):
    step = pl.program_id(0)
    part = first_ref.shape[-1]
    block = first_ref.shape[-2]

    def values(slot, x):
        cols = slice(x * part, (x + 1) * part)
        codes = codes_ref[slot * block:(slot + 1) * block, cols].astype(jnp.float32)
        return (codes * scales_ref[slot:slot + 1, cols]).astype(jnp.bfloat16)

    for x in range(RING):
        first_ref[x, 0] = values(0, x)
    for s, ref in enumerate(second_refs):
        @pl.when(step == s)
        def _():
            for x in range(RING):
                ref[x] = values(1, x)


def dequantize(codes, scales, z):
    capacity, width = codes.shape
    slots, col_blocks = scales.shape
    block = capacity // slots
    quarter = width // RING
    part = quarter // RING
    spread = jnp.repeat(scales.astype(jnp.float32), width // col_blocks, axis=1)
    return pl.pallas_call(
        dequantize_kernel,
        grid_spec=pltpu.PrefetchScalarGridSpec(
            num_scalar_prefetch=1,
            grid=(RING,),
            in_specs=[
                pl.BlockSpec((capacity, quarter), lambda i, place: (0, place[0] ^ i)),
                pl.BlockSpec((slots, quarter), lambda i, place: (0, place[0] ^ i)),
            ],
            out_specs=[pl.BlockSpec((RING, 1, block, part), lambda i, place: (0, place[0] ^ i, 0, 0))]
            + [pl.BlockSpec((RING, block, part), lambda i, place: (0, 0, 0))] * RING,
        ),
        out_shape=[jax.ShapeDtypeStruct((RING, RING, block, part), jnp.bfloat16)]
        + [jax.ShapeDtypeStruct((RING, block, part), jnp.bfloat16)] * RING,
        compiler_params=PARAMS,
        name="dequantize",
    )(z[None], codes, spread)


def gather_kernel(kind_ref, index_ref, half_ref, *refs):
    sources, outs = refs[:6], refs[6:10]
    rows = math.gcd(outs[0].shape[0], sources[0].shape[1])
    count = outs[0].shape[0] // rows
    for s, out_ref in enumerate(outs):
        for i in range(count):
            n = s * count + i
            half = pl.ds(pl.multiple_of(half_ref[n] * rows, rows), rows)
            for kind, source in enumerate(sources):
                @pl.when(kind_ref[n] == kind)
                def _():
                    out_ref[i * rows:(i + 1) * rows, :] = source[index_ref[n], half, :]


def gather(kind, index, half, sources, hidden):
    part = sources[0].shape[-1]
    return pl.pallas_call(
        gather_kernel,
        grid_spec=pltpu.PrefetchScalarGridSpec(
            num_scalar_prefetch=3,
            grid=(1,),
            in_specs=[pl.BlockSpec(a.shape, lambda i, *_: (0, 0, 0)) for a in sources],
            out_specs=[pl.BlockSpec((hidden, part), lambda i, *_: (0, 0))] * RING,
        ),
        out_shape=[jax.ShapeDtypeStruct((hidden, part), sources[0].dtype)] * RING,
        compiler_params=PARAMS,
        name="gather_blocks",
    )(kind, index, half, *sources)


def together(*values):
    return lax.optimization_barrier(values)


def move(old_codes, old_scales, tokens, cotangent):
    y, x, z, c = (lax.axis_index(a) for a in AXES)
    first, *second = dequantize(old_codes, old_scales, z)
    tokens, *second = together(tokens, *second)
    tokens = all_to_all(cut_tokens(tokens, c, tokens.shape[0] // 2), "x")
    second = exchange(second, "z")
    first, tokens, cotangent, *second = together(first, tokens, cotangent, *second)
    first = all_to_all(first, "x")
    cot = jnp.stack(exchange([pick(cotangent, y ^ s) for s in range(RING)], "y"))
    second = jnp.stack(second, axis=1)
    first, second, cot = together(first, second, cot)
    firsts = exchange([pick(first, z ^ s, 1) for s in range(RING)], "z")
    second = all_to_all(second, "x")
    second, cot = together(second, cot)
    return lax.all_gather(tokens, ("y", "c")), firsts, second, cot


def weight_rows(firsts, second, old_offsets, local_hidden):
    y, x, z, c = (lax.axis_index(a) for a in AXES)
    owners = RING * RING
    slots = 2
    block, part = second.shape[-2:]
    hidden = local_hidden // RING

    give = [lax.dynamic_slice_in_dim(a, 2 * (1 - c), 2, 0) for a in firsts]
    give = give + [lax.dynamic_slice_in_dim(second, 2 * (1 - c), 2, 0).reshape(2 * RING, block, part)]
    other = lax.ppermute(jnp.concatenate(give), "c", [(0, 1), (1, 0)])

    group = 2 * y + c
    rows = math.gcd(hidden, block)
    count = hidden // rows
    n = jnp.arange(RING * count, dtype=jnp.int32)
    row = group * local_hidden + (z ^ (n // count)) * hidden + rows * (n % count)
    starts = old_offsets[:-1]
    before = (starts[None, :] <= row[:, None]).astype(jnp.int32)
    owner = jnp.sum(before, axis=1) - 1
    start = jnp.max(jnp.where(before == 1, starts[None, :], 0), axis=1)
    member = owner - group * owners
    low, zs, cs = member >> 3, (member >> 1) & 3, member & 1
    slot = (row - start) // block
    half = (row - start) % block // rows
    s = zs ^ z
    kind = jnp.where(cs != c, RING + 1, jnp.where(slot == 0, s, RING))
    index = jnp.where(
        cs != c,
        jnp.where(slot == 0, s * 2 + low, 2 * RING + low * RING + s),
        jnp.where(slot == 0, 2 * c + low, (2 * c + low) * RING + s),
    )
    sources = firsts + [second.reshape(owners, block, part), other]
    return gather(kind, index, half, sources, hidden)


def project_kernel(place_ref, tokens_ref, *refs):
    weights, outs, all_ref = refs[:RING], refs[RING:-1], refs[-1]
    step = pl.program_id(0)
    part = weights[0].shape[1]
    rows = outs[0].shape[2]

    @pl.when(step == 0)
    def _():
        for s, ref in enumerate(weights):
            all_ref[:, pl.ds(pl.multiple_of((place_ref[0] ^ s) * part, part), part)] = ref[...]

    product = lax.dot_general(
        all_ref[...], tokens_ref[...].reshape(RING * rows, RING * part),
        (((1,), (1,)), ((), ())), preferred_element_type=jnp.float32,
    ).astype(jnp.bfloat16)
    for n, ref in enumerate(outs):
        @pl.when(step == n)
        def _():
            for i in range(RING):
                ref[i] = product[:, i * rows:(i + 1) * rows]


def project(tokens, weights, positions, z):
    pieces, _, share, quarter = tokens.shape
    hidden, part = weights[0].shape
    rows = pieces * share // RING
    count = len(positions)
    return pl.pallas_call(
        project_kernel,
        grid_spec=pltpu.PrefetchScalarGridSpec(
            num_scalar_prefetch=1,
            grid=(count,),
            in_specs=[
                pl.BlockSpec((pieces, 1, share, quarter), lambda i, place: (0, place[1 + i], 0, 0))
            ]
            + [pl.BlockSpec((hidden, part), lambda i, place: (0, 0))] * RING,
            out_specs=[pl.BlockSpec((RING, hidden, rows), lambda i, place: (0, 0, 0))] * count,
            scratch_shapes=[pltpu.VMEM((hidden, quarter), jnp.bfloat16)],
        ),
        out_shape=[jax.ShapeDtypeStruct((RING, hidden, rows), jnp.bfloat16)] * count,
        compiler_params=PARAMS,
        name="project",
    )(jnp.stack([z, *positions]), tokens, *weights)


def grad_kernel(place_ref, tokens_ref, *refs):
    cots, outs, total_ref, cot_ref = refs[:RING], refs[RING:2 * RING], refs[2 * RING], refs[2 * RING + 1]
    step = pl.program_id(0)
    rows = cots[0].shape[2]
    part = outs[0].shape[1]
    for s, ref in enumerate(cots):
        @pl.when(step == s)
        def _():
            for t in range(RING):
                start = pl.multiple_of((place_ref[0] ^ t) * rows, rows)
                cot_ref[:, pl.ds(start, rows)] = ref[t]
    product = lax.dot_general(
        cot_ref[...], tokens_ref[...].reshape(cot_ref.shape[1], tokens_ref.shape[-1]),
        (((1,), (0,)), ((), ())), preferred_element_type=jnp.float32,
    )

    @pl.when(step == 0)
    def _():
        total_ref[...] = product

    @pl.when(step > 0)
    def _():
        total_ref[...] += product

    @pl.when(step == pl.num_programs(0) - 1)
    def _():
        for s, ref in enumerate(outs):
            start = pl.multiple_of((place_ref[0] ^ s) * part, part)
            ref[...] = total_ref[:, pl.ds(start, part)].astype(ref.dtype)


def gradient(tokens, cots, y, x):
    pieces, _, share, quarter = tokens.shape
    part = quarter // RING
    _, hidden, rows = cots[0].shape
    return pl.pallas_call(
        grad_kernel,
        grid_spec=pltpu.PrefetchScalarGridSpec(
            num_scalar_prefetch=1,
            grid=(RING,),
            in_specs=[pl.BlockSpec((pieces, 1, share, quarter), lambda i, place: (0, place[1] ^ i, 0, 0))]
            + [pl.BlockSpec((RING, hidden, rows), lambda i, place: (0, 0, 0))] * RING,
            out_specs=[pl.BlockSpec((hidden, part), lambda i, place: (0, 0))] * RING,
            scratch_shapes=[
                pltpu.VMEM((hidden, quarter), jnp.float32),
                pltpu.VMEM((hidden, RING * rows), jnp.bfloat16),
            ],
        ),
        out_shape=[jax.ShapeDtypeStruct((hidden, part), jnp.bfloat16)] * RING,
        compiler_params=PARAMS,
        name="gradient",
    )(jnp.stack([y, x]), tokens, *cots)


def assemble_kernel(place_ref, *refs):
    pieces, out_ref, all_ref = refs[:RING], refs[RING], refs[RING + 1]
    hidden = pieces[0].shape[0]
    for s, ref in enumerate(pieces):
        start = pl.multiple_of((place_ref[0] ^ s) * hidden, hidden)
        all_ref[pl.ds(start, hidden), :] = ref[...].astype(jnp.float32)
    out_ref[...] = all_ref[...].T.astype(out_ref.dtype)


def assemble(pieces, me, dtype):
    hidden, rows = pieces[0].shape
    lanes = min(rows, 128)
    return pl.pallas_call(
        assemble_kernel,
        grid_spec=pltpu.PrefetchScalarGridSpec(
            num_scalar_prefetch=1,
            grid=(rows // lanes,),
            in_specs=[pl.BlockSpec((hidden, lanes), lambda i, place: (0, i))] * RING,
            out_specs=pl.BlockSpec((lanes, RING * hidden), lambda i, place: (i, 0)),
            scratch_shapes=[pltpu.VMEM((RING * hidden, lanes), jnp.float32)],
        ),
        out_shape=jax.ShapeDtypeStruct((rows, RING * hidden), dtype),
        compiler_params=PARAMS,
        name="assemble",
    )(me[None], *pieces)


def on_device(old_codes, old_scales, old_offsets, tokens, cotangent):
    y, x, z, c = (lax.axis_index(a) for a in AXES)
    local_tokens, width = tokens.shape
    local_hidden = cotangent.shape[1]
    hidden = local_hidden // RING

    with jax.named_scope("move"):
        cut = cotangent.T.reshape(RING, hidden, local_tokens)
        every, firsts, second, cot = move(old_codes, old_scales, tokens, cut)

    with jax.named_scope("weight"):
        weights = exchange(weight_rows(firsts, second, old_offsets, local_hidden), "z")

    cots = exchange([cot] * RING, "x")
    sides = together(*weights, *cots)
    weights, cots = sides[:RING], sides[RING:]

    with jax.named_scope("projected"):
        far, right = project(every, weights, [x ^ 2, x ^ 1], z)
        left, own = project(every, weights, [x ^ 3, x], z)
        parts = [own, swap(far, "x", 2), swap(right, "x", 1), swap(left, "x", 3)]
        total = sum(p.astype(jnp.float32) for p in parts).astype(jnp.bfloat16)

    with jax.named_scope("grad"):
        grads = exchange(gradient(every, cots, y, x), "y")

    done = []
    for s in range(RING):
        pairs = [(a * RING + b, (b ^ s) * RING + a) for a in range(RING) for b in range(RING)]
        done.append(lax.ppermute(pick(total, z ^ s), ("y", "z"), pairs))
    return assemble(done, y, jnp.bfloat16), assemble(grads, y, jnp.float32)


def solution(mesh):
    devices = mesh.devices.reshape(RING, RING, RING, 2)
    split = Mesh(devices, AXES)
    fsdp, tp = ("y", "x"), ("z", "c")
    placed = (P(fsdp + tp, None), P(fsdp + tp, None), P(), P(fsdp, None), P(fsdp, tp))
    return jax.shard_map(
        on_device,
        mesh=split,
        in_specs=placed,
        out_specs=(P(fsdp, tp), P(fsdp, tp)),
        check_vma=False,
    )
```

```python
import math

import jax
import jax.numpy as jnp
from jax import lax
from jax.experimental import pallas as pl
from jax.experimental.pallas import tpu as pltpu
from jax.sharding import Mesh, PartitionSpec as P

AXES = ("y", "x", "z", "c")
RING = 4
NEAR_LAST = (2, 1, 3)
PARAMS = pltpu.CompilerParams(vmem_limit_bytes=56 << 20)


def swap(array, axis, s):
    return lax.ppermute(array, axis, [(i, i ^ s) for i in range(RING)])


def exchange(parts, axis):
    got = [parts[0]] + [None] * (RING - 1)
    for s in NEAR_LAST:
        got[s] = swap(parts[s], axis, s)
    return got


def pick(array, index, axis=0):
    return lax.dynamic_index_in_dim(array, index, axis, keepdims=False)


def all_to_all(array, axis):
    return lax.all_to_all(array, axis, 0, 0, tiled=True)


def cut_kernel(place_ref, tokens_ref, out_ref):
    part = out_ref.shape[2]
    for x in range(RING):
        out_ref[x] = tokens_ref[:, x * part:(x + 1) * part]


def cut_tokens(tokens, place, rows):
    width = tokens.shape[1]
    quarter = width // RING
    part = quarter // RING
    return pl.pallas_call(
        cut_kernel,
        grid_spec=pltpu.PrefetchScalarGridSpec(
            num_scalar_prefetch=1,
            grid=(RING,),
            in_specs=[pl.BlockSpec((rows, quarter), lambda q, place: (place[0], q))],
            out_specs=pl.BlockSpec((RING, rows, part), lambda q, place: (0, 0, q)),
        ),
        out_shape=jax.ShapeDtypeStruct((RING, rows, quarter), tokens.dtype),
        compiler_params=PARAMS,
        name="cut_tokens",
    )(place[None], tokens)


def dequantize_kernel(place_ref, codes_ref, scales_ref, first_ref, *second_refs):
    step = pl.program_id(0)
    part = first_ref.shape[-1]
    block = first_ref.shape[-2]

    def values(slot, x):
        cols = slice(x * part, (x + 1) * part)
        codes = codes_ref[slot * block:(slot + 1) * block, cols].astype(jnp.float32)
        return (codes * scales_ref[slot:slot + 1, cols]).astype(jnp.bfloat16)

    for x in range(RING):
        first_ref[x, 0] = values(0, x)
    for s, ref in enumerate(second_refs):
        @pl.when(step == s)
        def _():
            for x in range(RING):
                ref[x] = values(1, x)


def dequantize(codes, scales, z):
    capacity, width = codes.shape
    slots, col_blocks = scales.shape
    block = capacity // slots
    quarter = width // RING
    part = quarter // RING
    spread = jnp.repeat(scales.astype(jnp.float32), width // col_blocks, axis=1)
    return pl.pallas_call(
        dequantize_kernel,
        grid_spec=pltpu.PrefetchScalarGridSpec(
            num_scalar_prefetch=1,
            grid=(RING,),
            in_specs=[
                pl.BlockSpec((capacity, quarter), lambda i, place: (0, place[0] ^ i)),
                pl.BlockSpec((slots, quarter), lambda i, place: (0, place[0] ^ i)),
            ],
            out_specs=[pl.BlockSpec((RING, 1, block, part), lambda i, place: (0, place[0] ^ i, 0, 0))]
            + [pl.BlockSpec((RING, block, part), lambda i, place: (0, 0, 0))] * RING,
        ),
        out_shape=[jax.ShapeDtypeStruct((RING, RING, block, part), jnp.bfloat16)]
        + [jax.ShapeDtypeStruct((RING, block, part), jnp.bfloat16)] * RING,
        compiler_params=PARAMS,
        name="dequantize",
    )(z[None], codes, spread)


def gather_kernel(kind_ref, index_ref, half_ref, *refs):
    sources, outs = refs[:6], refs[6:10]
    rows = math.gcd(outs[0].shape[0], sources[0].shape[1])
    count = outs[0].shape[0] // rows
    for s, out_ref in enumerate(outs):
        for i in range(count):
            n = s * count + i
            half = pl.ds(pl.multiple_of(half_ref[n] * rows, rows), rows)
            for kind, source in enumerate(sources):
                @pl.when(kind_ref[n] == kind)
                def _():
                    out_ref[i * rows:(i + 1) * rows, :] = source[index_ref[n], half, :]


def gather(kind, index, half, sources, hidden):
    part = sources[0].shape[-1]
    return pl.pallas_call(
        gather_kernel,
        grid_spec=pltpu.PrefetchScalarGridSpec(
            num_scalar_prefetch=3,
            grid=(1,),
            in_specs=[pl.BlockSpec(a.shape, lambda i, *_: (0, 0, 0)) for a in sources],
            out_specs=[pl.BlockSpec((hidden, part), lambda i, *_: (0, 0))] * RING,
        ),
        out_shape=[jax.ShapeDtypeStruct((hidden, part), sources[0].dtype)] * RING,
        compiler_params=PARAMS,
        name="gather_blocks",
    )(kind, index, half, *sources)


def together(*values):
    return lax.optimization_barrier(values)


def stack_kernel(*refs):
    for s, ref in enumerate(refs[:-1]):
        refs[-1][0, s] = ref[0]


def stack(parts):
    count, rows, cols = parts[0].shape
    return pl.pallas_call(
        stack_kernel,
        grid=(count,),
        in_specs=[pl.BlockSpec((1, rows, cols), lambda i: (i, 0, 0))] * len(parts),
        out_specs=pl.BlockSpec((1, len(parts), rows, cols), lambda i: (i, 0, 0, 0)),
        out_shape=jax.ShapeDtypeStruct((count, len(parts), rows, cols), parts[0].dtype),
        compiler_params=PARAMS,
        name="stack",
    )(*parts)


def move(old_codes, old_scales, tokens, cotangent):
    y, x, z, c = (lax.axis_index(a) for a in AXES)
    first, *second = dequantize(old_codes, old_scales, z)
    tokens, *second = together(tokens, *second)
    tokens = all_to_all(cut_tokens(tokens, c, tokens.shape[0] // 2), "x")
    second = exchange(second, "z")
    first, tokens, cotangent, *second = together(first, tokens, cotangent, *second)
    first = all_to_all(first, "x")
    cot = jnp.stack(exchange([pick(cotangent, y ^ s) for s in range(RING)], "y"))
    first, second, cot = together(first, stack(second), cot)
    firsts = exchange([pick(first, z ^ s, 1) for s in range(RING)], "z")
    second = all_to_all(second, "x")
    second, cot = together(second, cot)
    return lax.all_gather(tokens, ("y", "c")), firsts, second, cot


def weight_rows(firsts, second, old_offsets, local_hidden):
    y, x, z, c = (lax.axis_index(a) for a in AXES)
    owners = RING * RING
    slots = 2
    block, part = second.shape[-2:]
    hidden = local_hidden // RING

    give = [lax.dynamic_slice_in_dim(a, 2 * (1 - c), 2, 0) for a in firsts]
    give = give + [lax.dynamic_slice_in_dim(second, 2 * (1 - c), 2, 0).reshape(2 * RING, block, part)]
    other = lax.ppermute(jnp.concatenate(give), "c", [(0, 1), (1, 0)])

    group = 2 * y + c
    rows = math.gcd(hidden, block)
    count = hidden // rows
    n = jnp.arange(RING * count, dtype=jnp.int32)
    row = group * local_hidden + (z ^ (n // count)) * hidden + rows * (n % count)
    starts = old_offsets[:-1]
    before = (starts[None, :] <= row[:, None]).astype(jnp.int32)
    owner = jnp.sum(before, axis=1) - 1
    start = jnp.max(jnp.where(before == 1, starts[None, :], 0), axis=1)
    member = owner - group * owners
    low, zs, cs = member >> 3, (member >> 1) & 3, member & 1
    slot = (row - start) // block
    half = (row - start) % block // rows
    s = zs ^ z
    kind = jnp.where(cs != c, RING + 1, jnp.where(slot == 0, s, RING))
    index = jnp.where(
        cs != c,
        jnp.where(slot == 0, s * 2 + low, 2 * RING + low * RING + s),
        jnp.where(slot == 0, 2 * c + low, (2 * c + low) * RING + s),
    )
    sources = firsts + [second.reshape(owners, block, part), other]
    return gather(kind, index, half, sources, hidden)


def project_kernel(place_ref, tokens_ref, *refs):
    weights, outs, all_ref = refs[:RING], refs[RING:-1], refs[-1]
    step = pl.program_id(0)
    part = weights[0].shape[1]
    rows = outs[0].shape[2]

    @pl.when(step == 0)
    def _():
        for s, ref in enumerate(weights):
            all_ref[:, pl.ds(pl.multiple_of((place_ref[0] ^ s) * part, part), part)] = ref[...]

    product = lax.dot_general(
        all_ref[...], tokens_ref[...].reshape(RING * rows, RING * part),
        (((1,), (1,)), ((), ())), preferred_element_type=jnp.float32,
    ).astype(jnp.bfloat16)
    for n, ref in enumerate(outs):
        @pl.when(step == n)
        def _():
            for i in range(RING):
                ref[i] = product[:, i * rows:(i + 1) * rows]


def project(tokens, weights, positions, z):
    pieces, _, share, quarter = tokens.shape
    hidden, part = weights[0].shape
    rows = pieces * share // RING
    count = len(positions)
    return pl.pallas_call(
        project_kernel,
        grid_spec=pltpu.PrefetchScalarGridSpec(
            num_scalar_prefetch=1,
            grid=(count,),
            in_specs=[
                pl.BlockSpec((pieces, 1, share, quarter), lambda i, place: (0, place[1 + i], 0, 0))
            ]
            + [pl.BlockSpec((hidden, part), lambda i, place: (0, 0))] * RING,
            out_specs=[pl.BlockSpec((RING, hidden, rows), lambda i, place: (0, 0, 0))] * count,
            scratch_shapes=[pltpu.VMEM((hidden, quarter), jnp.bfloat16)],
        ),
        out_shape=[jax.ShapeDtypeStruct((RING, hidden, rows), jnp.bfloat16)] * count,
        compiler_params=PARAMS,
        name="project",
    )(jnp.stack([z, *positions]), tokens, *weights)


def grad_kernel(place_ref, tokens_ref, *refs):
    cots, outs, total_ref, cot_ref = refs[:RING], refs[RING:2 * RING], refs[2 * RING], refs[2 * RING + 1]
    step = pl.program_id(0)
    rows = cots[0].shape[2]
    part = outs[0].shape[1]
    for s, ref in enumerate(cots):
        @pl.when(step == s)
        def _():
            for t in range(RING):
                start = pl.multiple_of((place_ref[0] ^ t) * rows, rows)
                cot_ref[:, pl.ds(start, rows)] = ref[t]
    product = lax.dot_general(
        cot_ref[...], tokens_ref[...].reshape(cot_ref.shape[1], tokens_ref.shape[-1]),
        (((1,), (0,)), ((), ())), preferred_element_type=jnp.float32,
    )

    @pl.when(step == 0)
    def _():
        total_ref[...] = product

    @pl.when(step > 0)
    def _():
        total_ref[...] += product

    @pl.when(step == pl.num_programs(0) - 1)
    def _():
        for s, ref in enumerate(outs):
            start = pl.multiple_of((place_ref[0] ^ s) * part, part)
            ref[...] = total_ref[:, pl.ds(start, part)].astype(ref.dtype)


def gradient(tokens, cots, y, x):
    pieces, _, share, quarter = tokens.shape
    part = quarter // RING
    _, hidden, rows = cots[0].shape
    return pl.pallas_call(
        grad_kernel,
        grid_spec=pltpu.PrefetchScalarGridSpec(
            num_scalar_prefetch=1,
            grid=(RING,),
            in_specs=[pl.BlockSpec((pieces, 1, share, quarter), lambda i, place: (0, place[1] ^ i, 0, 0))]
            + [pl.BlockSpec((RING, hidden, rows), lambda i, place: (0, 0, 0))] * RING,
            out_specs=[pl.BlockSpec((hidden, part), lambda i, place: (0, 0))] * RING,
            scratch_shapes=[
                pltpu.VMEM((hidden, quarter), jnp.float32),
                pltpu.VMEM((hidden, RING * rows), jnp.bfloat16),
            ],
        ),
        out_shape=[jax.ShapeDtypeStruct((hidden, part), jnp.bfloat16)] * RING,
        compiler_params=PARAMS,
        name="gradient",
    )(jnp.stack([y, x]), tokens, *cots)


def assemble_kernel(place_ref, *refs):
    pieces, out_ref, all_ref = refs[:RING], refs[RING], refs[RING + 1]
    hidden = pieces[0].shape[0]
    for s, ref in enumerate(pieces):
        start = pl.multiple_of((place_ref[0] ^ s) * hidden, hidden)
        all_ref[pl.ds(start, hidden), :] = ref[...].astype(jnp.float32)
    out_ref[...] = all_ref[...].T.astype(out_ref.dtype)


def assemble(pieces, me, dtype):
    hidden, rows = pieces[0].shape
    lanes = min(rows, 128)
    return pl.pallas_call(
        assemble_kernel,
        grid_spec=pltpu.PrefetchScalarGridSpec(
            num_scalar_prefetch=1,
            grid=(rows // lanes,),
            in_specs=[pl.BlockSpec((hidden, lanes), lambda i, place: (0, i))] * RING,
            out_specs=pl.BlockSpec((lanes, RING * hidden), lambda i, place: (i, 0)),
            scratch_shapes=[pltpu.VMEM((RING * hidden, lanes), jnp.float32)],
        ),
        out_shape=jax.ShapeDtypeStruct((rows, RING * hidden), dtype),
        compiler_params=PARAMS,
        name="assemble",
    )(me[None], *pieces)


def on_device(old_codes, old_scales, old_offsets, tokens, cotangent):
    y, x, z, c = (lax.axis_index(a) for a in AXES)
    local_tokens, width = tokens.shape
    local_hidden = cotangent.shape[1]
    hidden = local_hidden // RING

    with jax.named_scope("move"):
        cut = cotangent.T.reshape(RING, hidden, local_tokens)
        every, firsts, second, cot = move(old_codes, old_scales, tokens, cut)

    with jax.named_scope("weight"):
        weights = exchange(weight_rows(firsts, second, old_offsets, local_hidden), "z")

    cots = exchange([cot] * RING, "x")
    sides = together(*weights, *cots)
    weights, cots = sides[:RING], sides[RING:]

    with jax.named_scope("projected"):
        far, right = project(every, weights, [x ^ 2, x ^ 1], z)
        left, own = project(every, weights, [x ^ 3, x], z)
        parts = [own, swap(far, "x", 2), swap(right, "x", 1), swap(left, "x", 3)]
        total = sum(p.astype(jnp.float32) for p in parts).astype(jnp.bfloat16)

    with jax.named_scope("grad"):
        grads = exchange(gradient(every, cots, y, x), "y")

    done = []
    for s in range(RING):
        pairs = [(a * RING + b, (b ^ s) * RING + a) for a in range(RING) for b in range(RING)]
        done.append(lax.ppermute(pick(total, z ^ s), ("y", "z"), pairs))
    return assemble(done, y, jnp.bfloat16), assemble(grads, y, jnp.float32)


def solution(mesh):
    devices = mesh.devices.reshape(RING, RING, RING, 2)
    split = Mesh(devices, AXES)
    fsdp, tp = ("y", "x"), ("z", "c")
    placed = (P(fsdp + tp, None), P(fsdp + tp, None), P(), P(fsdp, None), P(fsdp, tp))
    return jax.shard_map(
        on_device,
        mesh=split,
        in_specs=placed,
        out_specs=(P(fsdp, tp), P(fsdp, tp)),
        check_vma=False,
    )
```

```python
import math

import jax
import jax.numpy as jnp
from jax import lax
from jax.experimental import pallas as pl
from jax.experimental.pallas import tpu as pltpu
from jax.sharding import Mesh, PartitionSpec as P

AXES = ("y", "x", "z", "c")
RING = 4
NEAR_LAST = (2, 1, 3)
PARAMS = pltpu.CompilerParams(vmem_limit_bytes=56 << 20)


def swap(array, axis, s):
    return lax.ppermute(array, axis, [(i, i ^ s) for i in range(RING)])


def exchange(parts, axis):
    got = [parts[0]] + [None] * (RING - 1)
    for s in NEAR_LAST:
        got[s] = swap(parts[s], axis, s)
    return got


def pick(array, index, axis=0):
    return lax.dynamic_index_in_dim(array, index, axis, keepdims=False)


def all_to_all(array, axis):
    return lax.all_to_all(array, axis, 0, 0, tiled=True)


def cut_kernel(place_ref, tokens_ref, out_ref):
    part = out_ref.shape[2]
    for x in range(RING):
        out_ref[x] = tokens_ref[:, x * part:(x + 1) * part]


def cut_tokens(tokens, place, rows):
    width = tokens.shape[1]
    quarter = width // RING
    part = quarter // RING
    return pl.pallas_call(
        cut_kernel,
        grid_spec=pltpu.PrefetchScalarGridSpec(
            num_scalar_prefetch=1,
            grid=(RING,),
            in_specs=[pl.BlockSpec((rows, quarter), lambda q, place: (place[0], q))],
            out_specs=pl.BlockSpec((RING, rows, part), lambda q, place: (0, 0, q)),
        ),
        out_shape=jax.ShapeDtypeStruct((RING, rows, quarter), tokens.dtype),
        compiler_params=PARAMS,
        name="cut_tokens",
    )(place[None], tokens)


def dequantize_kernel(place_ref, codes_ref, scales_ref, first_ref, *second_refs):
    step = pl.program_id(0)
    part = first_ref.shape[-1]
    block = first_ref.shape[-2]

    def values(slot, x):
        cols = slice(x * part, (x + 1) * part)
        codes = codes_ref[slot * block:(slot + 1) * block, cols].astype(jnp.float32)
        return (codes * scales_ref[slot:slot + 1, cols]).astype(jnp.bfloat16)

    for x in range(RING):
        first_ref[x, 0] = values(0, x)
    for s, ref in enumerate(second_refs):
        @pl.when(step == s)
        def _():
            for x in range(RING):
                ref[x] = values(1, x)


def dequantize(codes, scales, z):
    capacity, width = codes.shape
    slots, col_blocks = scales.shape
    block = capacity // slots
    quarter = width // RING
    part = quarter // RING
    spread = jnp.repeat(scales.astype(jnp.float32), width // col_blocks, axis=1)
    return pl.pallas_call(
        dequantize_kernel,
        grid_spec=pltpu.PrefetchScalarGridSpec(
            num_scalar_prefetch=1,
            grid=(RING,),
            in_specs=[
                pl.BlockSpec((capacity, quarter), lambda i, place: (0, place[0] ^ i)),
                pl.BlockSpec((slots, quarter), lambda i, place: (0, place[0] ^ i)),
            ],
            out_specs=[pl.BlockSpec((RING, 1, block, part), lambda i, place: (0, place[0] ^ i, 0, 0))]
            + [pl.BlockSpec((RING, block, part), lambda i, place: (0, 0, 0))] * RING,
        ),
        out_shape=[jax.ShapeDtypeStruct((RING, RING, block, part), jnp.bfloat16)]
        + [jax.ShapeDtypeStruct((RING, block, part), jnp.bfloat16)] * RING,
        compiler_params=PARAMS,
        name="dequantize",
    )(z[None], codes, spread)


def gather_kernel(kind_ref, index_ref, half_ref, *refs):
    sources, outs = refs[:6], refs[6:10]
    rows = math.gcd(outs[0].shape[0], sources[0].shape[1])
    count = outs[0].shape[0] // rows
    for s, out_ref in enumerate(outs):
        for i in range(count):
            n = s * count + i
            half = pl.ds(pl.multiple_of(half_ref[n] * rows, rows), rows)
            for kind, source in enumerate(sources):
                @pl.when(kind_ref[n] == kind)
                def _():
                    out_ref[i * rows:(i + 1) * rows, :] = source[index_ref[n], half, :]


def gather(kind, index, half, sources, hidden):
    part = sources[0].shape[-1]
    return pl.pallas_call(
        gather_kernel,
        grid_spec=pltpu.PrefetchScalarGridSpec(
            num_scalar_prefetch=3,
            grid=(1,),
            in_specs=[pl.BlockSpec(a.shape, lambda i, *_: (0, 0, 0)) for a in sources],
            out_specs=[pl.BlockSpec((hidden, part), lambda i, *_: (0, 0))] * RING,
        ),
        out_shape=[jax.ShapeDtypeStruct((hidden, part), sources[0].dtype)] * RING,
        compiler_params=PARAMS,
        name="gather_blocks",
    )(kind, index, half, *sources)


def together(*values):
    return lax.optimization_barrier(values)


def stack_kernel(*refs):
    for s, ref in enumerate(refs[:-1]):
        refs[-1][0, s] = ref[0]


def stack(parts):
    count, rows, cols = parts[0].shape
    return pl.pallas_call(
        stack_kernel,
        grid=(count,),
        in_specs=[pl.BlockSpec((1, rows, cols), lambda i: (i, 0, 0))] * len(parts),
        out_specs=pl.BlockSpec((1, len(parts), rows, cols), lambda i: (i, 0, 0, 0)),
        out_shape=jax.ShapeDtypeStruct((count, len(parts), rows, cols), parts[0].dtype),
        compiler_params=PARAMS,
        name="stack",
    )(*parts)


def move(old_codes, old_scales, tokens, cotangent):
    y, x, z, c = (lax.axis_index(a) for a in AXES)
    first, *second = dequantize(old_codes, old_scales, z)
    tokens, *second = together(tokens, *second)
    tokens = all_to_all(cut_tokens(tokens, c, tokens.shape[0] // 2), "x")
    second = exchange(second, "z")
    first, tokens, cotangent, *second = together(first, tokens, cotangent, *second)
    first = all_to_all(first, "x")
    cot = jnp.stack(exchange([pick(cotangent, y ^ s) for s in range(RING)], "y"))
    first, second, cot = together(first, stack(second), cot)
    firsts = exchange([pick(first, z ^ s, 1) for s in range(RING)], "z")
    second = all_to_all(second, "x")
    second, cot = together(second, cot)
    return lax.all_gather(tokens, ("y", "c")), firsts, second, cot


def weight_rows(firsts, second, old_offsets, local_hidden):
    y, x, z, c = (lax.axis_index(a) for a in AXES)
    owners = RING * RING
    slots = 2
    block, part = second.shape[-2:]
    hidden = local_hidden // RING

    give = [lax.dynamic_slice_in_dim(a, 2 * (1 - c), 2, 0) for a in firsts]
    give = give + [lax.dynamic_slice_in_dim(second, 2 * (1 - c), 2, 0).reshape(2 * RING, block, part)]
    other = lax.ppermute(jnp.concatenate(give), "c", [(0, 1), (1, 0)])

    group = 2 * y + c
    rows = math.gcd(hidden, block)
    count = hidden // rows
    n = jnp.arange(RING * count, dtype=jnp.int32)
    row = group * local_hidden + (z ^ (n // count)) * hidden + rows * (n % count)
    starts = old_offsets[:-1]
    before = (starts[None, :] <= row[:, None]).astype(jnp.int32)
    owner = jnp.sum(before, axis=1) - 1
    start = jnp.max(jnp.where(before == 1, starts[None, :], 0), axis=1)
    member = owner - group * owners
    low, zs, cs = member >> 3, (member >> 1) & 3, member & 1
    slot = (row - start) // block
    half = (row - start) % block // rows
    s = zs ^ z
    kind = jnp.where(cs != c, RING + 1, jnp.where(slot == 0, s, RING))
    index = jnp.where(
        cs != c,
        jnp.where(slot == 0, s * 2 + low, 2 * RING + low * RING + s),
        jnp.where(slot == 0, 2 * c + low, (2 * c + low) * RING + s),
    )
    sources = firsts + [second.reshape(owners, block, part), other]
    return list(gather(kind, index, half, sources, hidden))


def project_kernel(place_ref, tokens_ref, *refs):
    weights, outs, all_ref = refs[:RING], refs[RING:-1], refs[-1]
    step = pl.program_id(0)
    part = weights[0].shape[1]
    rows = outs[0].shape[2]

    @pl.when(step == 0)
    def _():
        for s, ref in enumerate(weights):
            all_ref[:, pl.ds(pl.multiple_of((place_ref[0] ^ s) * part, part), part)] = ref[...]

    product = lax.dot_general(
        all_ref[...], tokens_ref[...].reshape(RING * rows, RING * part),
        (((1,), (1,)), ((), ())), preferred_element_type=jnp.float32,
    ).astype(jnp.bfloat16)
    for n, ref in enumerate(outs):
        @pl.when(step == n)
        def _():
            for i in range(RING):
                ref[i] = product[:, i * rows:(i + 1) * rows]


def project(tokens, weights, positions, z):
    pieces, _, share, quarter = tokens.shape
    hidden, part = weights[0].shape
    rows = pieces * share // RING
    count = len(positions)
    return pl.pallas_call(
        project_kernel,
        grid_spec=pltpu.PrefetchScalarGridSpec(
            num_scalar_prefetch=1,
            grid=(count,),
            in_specs=[
                pl.BlockSpec((pieces, 1, share, quarter), lambda i, place: (0, place[1 + i], 0, 0))
            ]
            + [pl.BlockSpec((hidden, part), lambda i, place: (0, 0))] * RING,
            out_specs=[pl.BlockSpec((RING, hidden, rows), lambda i, place: (0, 0, 0))] * count,
            scratch_shapes=[pltpu.VMEM((hidden, quarter), jnp.bfloat16)],
        ),
        out_shape=[jax.ShapeDtypeStruct((RING, hidden, rows), jnp.bfloat16)] * count,
        compiler_params=PARAMS,
        name="project",
    )(jnp.stack([z, *positions]), tokens, *weights)


def grad_kernel(place_ref, tokens_ref, *refs):
    cots, outs, total_ref, cot_ref = refs[:RING], refs[RING:2 * RING], refs[2 * RING], refs[2 * RING + 1]
    step = pl.program_id(0)
    rows = cots[0].shape[2]
    part = outs[0].shape[1]
    for s, ref in enumerate(cots):
        @pl.when(step == s)
        def _():
            for t in range(RING):
                start = pl.multiple_of((place_ref[0] ^ t) * rows, rows)
                cot_ref[:, pl.ds(start, rows)] = ref[t]
    product = lax.dot_general(
        cot_ref[...], tokens_ref[...].reshape(cot_ref.shape[1], tokens_ref.shape[-1]),
        (((1,), (0,)), ((), ())), preferred_element_type=jnp.float32,
    )

    @pl.when(step == 0)
    def _():
        total_ref[...] = product

    @pl.when(step > 0)
    def _():
        total_ref[...] += product

    @pl.when(step == pl.num_programs(0) - 1)
    def _():
        for s, ref in enumerate(outs):
            start = pl.multiple_of((place_ref[0] ^ s) * part, part)
            ref[...] = total_ref[:, pl.ds(start, part)].astype(ref.dtype)


def gradient(tokens, cots, y, x):
    pieces, _, share, quarter = tokens.shape
    part = quarter // RING
    _, hidden, rows = cots[0].shape
    return pl.pallas_call(
        grad_kernel,
        grid_spec=pltpu.PrefetchScalarGridSpec(
            num_scalar_prefetch=1,
            grid=(RING,),
            in_specs=[pl.BlockSpec((pieces, 1, share, quarter), lambda i, place: (0, place[1] ^ i, 0, 0))]
            + [pl.BlockSpec((RING, hidden, rows), lambda i, place: (0, 0, 0))] * RING,
            out_specs=[pl.BlockSpec((hidden, part), lambda i, place: (0, 0))] * RING,
            scratch_shapes=[
                pltpu.VMEM((hidden, quarter), jnp.float32),
                pltpu.VMEM((hidden, RING * rows), jnp.bfloat16),
            ],
        ),
        out_shape=[jax.ShapeDtypeStruct((hidden, part), jnp.bfloat16)] * RING,
        compiler_params=PARAMS,
        name="gradient",
    )(jnp.stack([y, x]), tokens, *cots)


def assemble_kernel(place_ref, *refs):
    pieces, out_ref, all_ref = refs[:RING], refs[RING], refs[RING + 1]
    hidden = pieces[0].shape[0]
    for s, ref in enumerate(pieces):
        start = pl.multiple_of((place_ref[0] ^ s) * hidden, hidden)
        all_ref[pl.ds(start, hidden), :] = ref[...].astype(jnp.float32)
    out_ref[...] = all_ref[...].T.astype(out_ref.dtype)


def assemble(pieces, me, dtype):
    hidden, rows = pieces[0].shape
    lanes = min(rows, 128)
    return pl.pallas_call(
        assemble_kernel,
        grid_spec=pltpu.PrefetchScalarGridSpec(
            num_scalar_prefetch=1,
            grid=(rows // lanes,),
            in_specs=[pl.BlockSpec((hidden, lanes), lambda i, place: (0, i))] * RING,
            out_specs=pl.BlockSpec((lanes, RING * hidden), lambda i, place: (i, 0)),
            scratch_shapes=[pltpu.VMEM((RING * hidden, lanes), jnp.float32)],
        ),
        out_shape=jax.ShapeDtypeStruct((rows, RING * hidden), dtype),
        compiler_params=PARAMS,
        name="assemble",
    )(me[None], *pieces)


def on_device(old_codes, old_scales, old_offsets, tokens, cotangent):
    y, x, z, c = (lax.axis_index(a) for a in AXES)
    local_tokens, width = tokens.shape
    local_hidden = cotangent.shape[1]
    hidden = local_hidden // RING

    with jax.named_scope("move"):
        cut = cotangent.T.reshape(RING, hidden, local_tokens)
        every, firsts, second, cot = move(old_codes, old_scales, tokens, cut)

    with jax.named_scope("weight"):
        rows = weight_rows(firsts, second, old_offsets, local_hidden)
        rows[0], last = together(rows[0], cot)
        weights = exchange(rows, "z")

    cots = [cot, swap(cot, "x", 1), swap(cot, "x", 2), swap(last, "x", 3)]
    sides = together(*weights, *cots[1:3])
    weights, cots[1:3] = sides[:RING], sides[RING:]

    with jax.named_scope("projected"):
        far, right = project(every, weights, [x ^ 2, x ^ 1], z)
        left, own = project(every, weights, [x ^ 3, x], z)
        parts = [own, swap(far, "x", 2), swap(right, "x", 1), swap(left, "x", 3)]
        total = sum(p.astype(jnp.float32) for p in parts).astype(jnp.bfloat16)

    with jax.named_scope("grad"):
        grads = exchange(gradient(every, cots, y, x), "y")

    done = []
    for s in range(RING):
        pairs = [(a * RING + b, (b ^ s) * RING + a) for a in range(RING) for b in range(RING)]
        done.append(lax.ppermute(pick(total, z ^ s), ("y", "z"), pairs))
    return assemble(done, y, jnp.bfloat16), assemble(grads, y, jnp.float32)


def solution(mesh):
    devices = mesh.devices.reshape(RING, RING, RING, 2)
    split = Mesh(devices, AXES)
    fsdp, tp = ("y", "x"), ("z", "c")
    placed = (P(fsdp + tp, None), P(fsdp + tp, None), P(), P(fsdp, None), P(fsdp, tp))
    return jax.shard_map(
        on_device,
        mesh=split,
        in_specs=placed,
        out_specs=(P(fsdp, tp), P(fsdp, tp)),
        check_vma=False,
    )
```
